32 devices in a mesh: rows: 8 (over z, x), cols: 4 (over y, core).
Axes of the slice: x: 2, y: 2, z: 4, core: 2. Of those that a mesh axis runs over, the one named last changes fastest.
Arguments:
- kernel: float32 [16384, 16384], P('rows', 'cols'), may hold values from 0 to 2, as said below
- row_block: int32 [256], P('rows'), may hold values from 0 to 255, as said below
- panel_order: int32 [2], replicated, may hold values from 0 to 63, as said below
- samples: float32 [16384, 512], P('rows', 'cols'), may hold values from -6 to 6
Outputs:
- trailing: float32 [16384, 16384], P('rows', 'cols')
- factor: float32 [16384, 512], P('rows')
- solved: float32 [512, 512], P(None, 'cols')
- reduced_samples: float32 [16384, 512], P('rows', 'cols')
The draws below stay inside these ranges and needn't reach their ends.
Inputs may be any that keep to these rules, and one draw needn't show every extreme that they name: `row_block`: the stored row blocks of rows index i (stored blocks i * 32 to (i + 1) * 32 - 1) hold the global row blocks i + t * 8, t = 0 .. 31, each once, in some order. `panel_order`: the entries are distinct, and one of them is 63. `kernel`: in global row order the matrix is symmetric and positive definite, its smallest eigenvalue 0.25 or more.
All inputs are finite; a program needn't handle non-finite values.
Results may differ from the reference program's by a relative error of at most 0.0003.
Values sent between devices are 32-bit elements; how exact they have to be, the bound alone decides.
A program may use at most 320 MiB of HBM per device.

```python
import jax
import jax.numpy as jnp
from jax import lax

N = 16384
SAMPLES = 512
PW = 256
PANELS = 2
NBLK = 256
BPD = 32
NPB = 64


def block_layout(key):
    devices_rows = NBLK // BPD
    scores = jax.random.randint(jax.random.fold_in(key, 7), (devices_rows, BPD), 0, 1 << 20) * BPD
    scores = scores + jnp.arange(BPD, dtype=jnp.int32)[None, :]
    ranking = jnp.argsort(scores, axis=1).astype(jnp.int32)
    layout = jnp.arange(devices_rows, dtype=jnp.int32)[:, None] + devices_rows * ranking
    return layout.reshape(NBLK).astype(jnp.int32)


def draw_row_block(key, part):
    return block_layout(key)


def draw_panel_order(key, part):
    others = jax.random.permutation(jax.random.fold_in(key, 11), NPB - 1)[:PANELS - 1].astype(jnp.int32)
    joined = jnp.concatenate([jnp.full((1,), NPB - 1, jnp.int32), others], 0)
    place = jax.random.randint(jax.random.fold_in(key, 17), (), 0, PANELS)
    return jnp.roll(joined, place).astype(jnp.int32)


def draw_kernel(key, part):
    layout = block_layout(key)
    sites_key = jax.random.fold_in(key, 13)
    spots = jax.random.uniform(sites_key, (N, 2), jnp.float32)
    length_scale = 0.15
    nugget = 0.3
    block_rows = N // NBLK
    rows_at = (layout[:, None] * block_rows + jnp.arange(block_rows, dtype=jnp.int32)[None, :]).reshape(N)
    here = spots[rows_at]
    delta_x = here[:, 0:1] - spots[None, :, 0]
    delta_y = here[:, 1:2] - spots[None, :, 1]
    distance = jnp.sqrt(delta_x * delta_x + delta_y * delta_y)
    cover = jnp.exp(-distance / length_scale)
    same_site = (rows_at[:, None] == jnp.arange(N, dtype=jnp.int32)[None, :]).astype(jnp.float32)
    return (cover + nugget * same_site).astype(jnp.float32)


def steps_of(key, dims, split, low, high):
    level = 1.0
    for dim, parts in split:
        heights = jax.random.uniform(jax.random.fold_in(jax.random.fold_in(key, 6), dim), (parts,), jnp.float32, low / len(split), high / len(split))
        level = level * jnp.repeat(jnp.exp(heights), dims[dim] // parts).reshape((-1,) + (1,) * (len(dims) - 1 - dim))
    return level


def scatter_about(key, dims, deviation, bound, split=(), kind=jnp.bfloat16):
    entries = jax.random.normal(key, dims, jnp.float32) * deviation
    if len(split) > 0:
        entries = steps_of(key, dims, split, -0.22, 0.18) * entries
    return jnp.clip(entries, min=-bound, max=bound).astype(kind)


def setup_inputs(seed: int = 0) -> dict:
    key_list = jax.random.split(jax.random.key(seed), 5)
    kernel = draw_kernel(jax.random.fold_in(key_list[4], 71), 0)
    row_block = draw_row_block(jax.random.fold_in(key_list[4], 71), 0)
    panel_order = draw_panel_order(jax.random.fold_in(key_list[4], 71), 0)
    samples = scatter_about(key_list[3], (N, SAMPLES), 1.0, 6.0, ((0, 8), (1, 4)), jnp.float32)
    return dict(kernel=kernel, row_block=row_block, panel_order=panel_order, samples=samples)


EXACT = lax.Precision.HIGHEST

def to_global(array, row_block):
    blocks_all = row_block.shape[0]
    ranking = jnp.argsort(row_block).astype(jnp.int32)
    return jnp.take(array.reshape(blocks_all, -1, array.shape[1]), ranking, axis=0).reshape(array.shape)

def to_stored(array, row_block):
    blocks_all = row_block.shape[0]
    return jnp.take(array.reshape(blocks_all, -1, array.shape[1]), row_block, axis=0).reshape(array.shape)

def times_transposed(left_side, right_side):
    return lax.dot_general(left_side.astype(jnp.float32), right_side.astype(jnp.float32), (((1,), (1,)), ((), ())), precision=EXACT, preferred_element_type=jnp.float32)

def matmul_plain(left_side, right_side):
    return jnp.dot(left_side.astype(jnp.float32), right_side.astype(jnp.float32), precision=EXACT, preferred_element_type=jnp.float32)

def reference(kernel, row_block, panel_order, samples):
    matrix = to_global(kernel, row_block)
    right_side = to_global(samples, row_block)
    identity = jnp.eye(PW, dtype=jnp.float32)
    factors = []
    solutions = []
    for panel_step in range(PANELS):
        panel_start = (panel_order[panel_step] * PW).astype(jnp.int32)
        columns = lax.dynamic_slice_in_dim(matrix, panel_start, PW, 1)
        diagonal = lax.dynamic_slice_in_dim(columns, panel_start, PW, 0)
        lower_factor = jnp.linalg.cholesky(diagonal)
        inverse = jax.scipy.linalg.solve_triangular(lower_factor, identity, lower=True)
        factor_now = times_transposed(columns, inverse)
        panel_right = lax.dynamic_slice_in_dim(right_side, panel_start, PW, 0)
        solved_now = matmul_plain(inverse, panel_right)
        right_side = right_side - matmul_plain(factor_now, solved_now)
        matrix = matrix - times_transposed(factor_now, factor_now)
        factors.append(factor_now)
        solutions.append(solved_now)
    factor_all = jnp.concatenate(factors, 1)
    return (to_stored(matrix, row_block), to_stored(factor_all, row_block), jnp.concatenate(solutions, 0), to_stored(right_side, row_block))
```

```python
import functools

import jax
import jax.numpy as jnp
from jax import lax
from jax.experimental import pallas as pl
from jax.experimental.pallas import tpu as pltpu
from jax.sharding import PartitionSpec as P

PW = 256
PANELS = 2
WIDE = PW * PANELS
SUB = 128
STRIP = 8

EXACT = lax.Precision.HIGHEST


def eliminate(block):
    strips = [block[s * STRIP : (s + 1) * STRIP, :] for s in range(SUB // STRIP)]
    row_id = lax.broadcasted_iota(jnp.int32, (STRIP, SUB), 0)
    lane_id = lax.broadcasted_iota(jnp.int32, (STRIP, SUB), 1)
    right = [
        jnp.where(lane_id == row_id + s * STRIP, 1.0, 0.0).astype(jnp.float32)
        for s in range(SUB // STRIP)
    ]
    below = lax.broadcasted_iota(jnp.int32, (STRIP, 1), 0)
    pivots = [jnp.zeros((STRIP, 1), jnp.float32) for s in range(SUB // STRIP)]
    for col in range(SUB):
        home, place = divmod(col, STRIP)
        row_left = strips[home][place : place + 1, :]
        row_right = right[home][place : place + 1, :]
        pivot = row_left[:, col : col + 1]
        scale = 1.0 / pivot
        pivots[home] = jnp.where(below == place, pivot, pivots[home])
        scaled_left = row_left * scale
        scaled_right = row_right * scale
        for s in range(home, SUB // STRIP):
            if s == home and place == STRIP - 1:
                continue
            ratio = strips[s][:, col : col + 1]
            if s == home:
                ratio = jnp.where(below > place, ratio, 0.0)
            strips[s] = strips[s] - ratio * scaled_left
            right[s] = right[s] - ratio * scaled_right
    return jnp.concatenate(
        [right[s] * lax.rsqrt(pivots[s]) for s in range(SUB // STRIP)], axis=0
    )


def invert_kernel(diag_ref, out_ref, work):
    count = WIDE // SUB
    work[:, :WIDE] = diag_ref[...]
    rows = lax.broadcasted_iota(jnp.int32, (WIDE, WIDE), 0)
    lanes = lax.broadcasted_iota(jnp.int32, (WIDE, WIDE), 1)
    work[:, WIDE:] = jnp.where(rows == lanes, 1.0, 0.0).astype(jnp.float32)

    def step(k, carry):
        here = pl.ds(pl.multiple_of(k * SUB, SUB), SUB)
        inverse = eliminate(work[here, here])
        scaled = jnp.dot(
            inverse, work[here, :], precision=EXACT, preferred_element_type=jnp.float32
        )
        work[here, :] = scaled
        for i in range(1, count):

            @pl.when(i > k)
            def _():
                left = work[here, i * SUB : (i + 1) * SUB]
                work[i * SUB : (i + 1) * SUB, :] -= lax.dot_general(
                    left,
                    work[here, :],
                    (((0,), (0,)), ((), ())),
                    precision=EXACT,
                    preferred_element_type=jnp.float32,
                )

        return carry

    lax.fori_loop(0, count, step, 0)
    out_ref[...] = work[:, WIDE:]


def invert(diagonal):
    return pl.pallas_call(
        invert_kernel,
        out_shape=jax.ShapeDtypeStruct((WIDE, WIDE), jnp.float32),
        in_specs=[pl.BlockSpec(memory_space=pltpu.VMEM)],
        out_specs=pl.BlockSpec(memory_space=pltpu.VMEM),
        scratch_shapes=[pltpu.VMEM((WIDE, 2 * WIDE), jnp.float32)],
        compiler_params=pltpu.CompilerParams(vmem_limit_bytes=32 * 1024 * 1024),
        name="invert",
    )(diagonal)


def halves(value):
    high = value.astype(jnp.bfloat16)
    low = (value - high.astype(jnp.float32)).astype(jnp.bfloat16)
    return high, low


def times_transposed(left, right):
    return lax.dot_general(
        left,
        right,
        (((1,), (1,)), ((), ())),
        precision=EXACT,
        preferred_element_type=jnp.float32,
    )


def split_product(left, right):
    def one(a, b):
        return lax.dot_general(
            a, b, (((1,), (1,)), ((), ())), preferred_element_type=jnp.float32
        )

    return one(left[0], right[0]) + (one(left[0], right[1]) + one(left[1], right[0]))


def update_kernel(
    inverse_ref, wanted_ref, cols_ref, own_ref, kernel_ref, samples_ref,
    trailing_ref, factor_ref, solved_ref, reduced_ref,
    own_high, own_low, cols_high, cols_low,
):
    j = pl.program_id(0)
    i = pl.program_id(1)
    tile = kernel_ref.shape[0]
    at = pl.ds(pl.multiple_of(i * tile, tile), tile)

    @pl.when((i == 0) & (j == 0))
    def _():
        solved_ref[...] = jnp.dot(
            inverse_ref[...], wanted_ref[...], precision=EXACT, preferred_element_type=jnp.float32
        )

    @pl.when(i == 0)
    def _():
        high, low = halves(times_transposed(cols_ref[...], inverse_ref[...]))
        cols_high[...] = high
        cols_low[...] = low

    @pl.when(j == 0)
    def _():
        factor = times_transposed(own_ref[...], inverse_ref[...])
        factor_ref[...] = factor
        high, low = halves(factor)
        own_high[at, :] = high
        own_low[at, :] = low
        reduced_ref[...] = samples_ref[...] - jnp.dot(
            factor, solved_ref[...], precision=EXACT, preferred_element_type=jnp.float32
        )

    trailing_ref[...] = kernel_ref[...] - split_product(
        (own_high[at, :], own_low[at, :]), (cols_high[...], cols_low[...])
    )


def update(inverse, wanted, columns, own, kernel, samples):
    rows, width = kernel.shape
    right = samples.shape[1]
    tile = min(512, rows)
    span = min(1024, width)
    steps = rows // tile

    def first(j, i):
        return (jnp.where(j == 0, i, steps - 1), 0)

    return pl.pallas_call(
        update_kernel,
        grid=(width // span, steps),
        in_specs=[
            pl.BlockSpec((WIDE, WIDE), lambda j, i: (0, 0)),
            pl.BlockSpec((WIDE, right), lambda j, i: (0, 0)),
            pl.BlockSpec((span, WIDE), lambda j, i: (j, 0)),
            pl.BlockSpec((tile, WIDE), first),
            pl.BlockSpec((tile, span), lambda j, i: (i, j)),
            pl.BlockSpec((tile, right), first),
        ],
        out_specs=[
            pl.BlockSpec((tile, span), lambda j, i: (i, j)),
            pl.BlockSpec((tile, WIDE), first),
            pl.BlockSpec((WIDE, right), lambda j, i: (0, 0)),
            pl.BlockSpec((tile, right), first),
        ],
        out_shape=[
            jax.ShapeDtypeStruct((rows, width), jnp.float32),
            jax.ShapeDtypeStruct((rows, WIDE), jnp.float32),
            jax.ShapeDtypeStruct((WIDE, right), jnp.float32),
            jax.ShapeDtypeStruct((rows, right), jnp.float32),
        ],
        scratch_shapes=[
            pltpu.VMEM((rows, WIDE), jnp.bfloat16),
            pltpu.VMEM((rows, WIDE), jnp.bfloat16),
            pltpu.VMEM((span, WIDE), jnp.bfloat16),
            pltpu.VMEM((span, WIDE), jnp.bfloat16),
        ],
        compiler_params=pltpu.CompilerParams(vmem_limit_bytes=56 * 1024 * 1024),
        name="update",
    )(inverse, wanted, columns, own, kernel, samples)


def on_device(kernel, row_block, panel_order, samples):
    rows_count = lax.axis_size("rows")
    cols_count = lax.axis_size("cols")
    cols_place = lax.axis_index("cols")
    blocks_here = row_block.shape[0]
    local_rows, local_cols = kernel.shape
    block_rows = local_rows // blocks_here
    per_panel = PW // block_rows
    share = blocks_here // cols_count
    right_cols = samples.shape[1]
    ranking = jnp.argsort(row_block)

    picked = []
    wanted = []
    for step in range(PANELS):
        start = panel_order[step] * PW
        owner = start // local_cols
        part = lax.dynamic_slice_in_dim(kernel, start - owner * local_cols, PW, 1)
        picked.append(jnp.where(cols_place == owner, part, jnp.zeros_like(part)))
        wanted.append(panel_order[step] * per_panel + jnp.arange(per_panel, dtype=jnp.int32))
    own = lax.psum(jnp.concatenate(picked, 1), "cols")

    own_blocks = own.reshape(blocks_here, block_rows, WIDE)
    wanted = jnp.concatenate(wanted, 0)
    matches = wanted[:, None] == row_block[None, :]
    held = jnp.any(matches, 1)[:, None, None]
    where = jnp.argmax(matches, 1)
    diag_part = jnp.where(held, jnp.take(own_blocks, where, axis=0), 0.0).reshape(WIDE, WIDE)
    right_part = jnp.where(
        held,
        jnp.take(samples.reshape(blocks_here, block_rows, right_cols), where, axis=0),
        0.0,
    ).reshape(WIDE, right_cols)
    diagonal, panel_right = lax.psum((diag_part, right_part), "rows")

    mine = lax.dynamic_slice_in_dim(ranking, cols_place * share, share, 0)
    piece = jnp.take(own_blocks, mine, axis=0)
    columns = (
        lax.all_gather(piece, "rows", axis=0)
        .transpose(1, 0, 2, 3)
        .reshape(local_cols, WIDE)
    )

    inverse = invert(diagonal)
    return tuple(update(inverse, panel_right, columns, own, kernel, samples))


def solution(mesh):
    in_specs = (P("rows", "cols"), P("rows"), P(), P("rows", "cols"))
    out_specs = (P("rows", "cols"), P("rows", None), P(None, "cols"), P("rows", "cols"))
    return jax.shard_map(
        on_device, mesh=mesh, in_specs=in_specs, out_specs=out_specs, check_vma=False
    )
```

```python
import functools

import jax
import jax.numpy as jnp
from jax import lax
from jax.experimental import pallas as pl
from jax.experimental.pallas import tpu as pltpu
from jax.sharding import PartitionSpec as P

PW = 256
PANELS = 2
WIDE = PW * PANELS
SUB = 128
STRIP = 8

EXACT = lax.Precision.HIGHEST


def eliminate(block):
    rows = lax.broadcasted_iota(jnp.int32, (SUB, SUB), 0)
    lanes = lax.broadcasted_iota(jnp.int32, (SUB, SUB), 1)
    place = lax.broadcasted_iota(jnp.int32, (SUB, 1), 0)
    left = block
    right = jnp.where(rows == lanes, 1.0, 0.0).astype(jnp.float32)
    pivots = jnp.ones((SUB, 1), jnp.float32)
    for col in range(SUB):
        row_left = left[col : col + 1, :]
        pivot = row_left[:, col : col + 1]
        scale = 1.0 / pivot
        pivots = jnp.where(place == col, pivot, pivots)
        ratio = jnp.where(place > col, left[:, col : col + 1], 0.0)
        row_right = right[col : col + 1, :] * scale
        left = left - ratio * (row_left * scale)
        right = right - ratio * row_right
    return right * lax.rsqrt(pivots)


def invert_steps(work, between):
    count = WIDE // SUB
    rows = lax.broadcasted_iota(jnp.int32, (WIDE, WIDE), 0)
    lanes = lax.broadcasted_iota(jnp.int32, (WIDE, WIDE), 1)
    work[:, WIDE:] = jnp.where(rows == lanes, 1.0, 0.0).astype(jnp.float32)

    def step(k, carry):
        here = pl.ds(pl.multiple_of(k * SUB, SUB), SUB)
        inverse = eliminate(work[here, here])
        between(k, 0)
        work[here, :] = jnp.dot(
            inverse, work[here, :], precision=EXACT, preferred_element_type=jnp.float32
        )
        for i in range(1, count):

            @pl.when(i > k)
            def _():
                work[i * SUB : (i + 1) * SUB, :] -= lax.dot_general(
                    work[here, i * SUB : (i + 1) * SUB],
                    work[here, :],
                    (((0,), (0,)), ((), ())),
                    precision=EXACT,
                    preferred_element_type=jnp.float32,
                )

        between(k, 1)
        return carry

    lax.fori_loop(0, count, step, 0)


def invert_kernel(diag_ref, out_ref, work):
    work[:, :WIDE] = diag_ref[...]
    invert_steps(work, lambda k, turn: None)
    out_ref[...] = work[:, WIDE:]


def invert(diagonal):
    return pl.pallas_call(
        invert_kernel,
        out_shape=jax.ShapeDtypeStruct((WIDE, WIDE), jnp.float32),
        in_specs=[pl.BlockSpec(memory_space=pltpu.VMEM)],
        out_specs=pl.BlockSpec(memory_space=pltpu.VMEM),
        scratch_shapes=[pltpu.VMEM((WIDE, 2 * WIDE), jnp.float32)],
        compiler_params=pltpu.CompilerParams(vmem_limit_bytes=32 * 1024 * 1024),
        name="invert",
    )(diagonal)


def ring_index(position):
    turn = position // 4
    return 2 * (position + turn * (7 - 2 * position)) + turn


def exchange_kernel(
    parts_ref, diag_ref, right_ref,
    own_ref, columns_ref, wanted_ref, out_ref,
    parts_in, diag_in, diag_all, right_all, slabs, work,
    part_sem, diag_sem, row_sem, right_sem, slab_sem, own_sem, ring_sem,
):
    i = lax.axis_index("rows")
    j = lax.axis_index("cols")
    place = (i // 2) + (i % 2) * (7 - 2 * (i // 2))
    after = ring_index((place + 1) % 8)
    before = ring_index((place + 7) % 8)
    half = columns_ref.shape[1] // 2
    rights = right_ref.shape[1]
    block_rows = SUB // PANELS

    def to(src, dst, sems, row, col):
        return pltpu.make_async_remote_copy(
            src_ref=src, dst_ref=dst, send_sem=sems.at[0], recv_sem=sems.at[1],
            device_id=(row, col), device_id_type=pl.DeviceIdType.MESH,
        )

    barrier = pltpu.get_barrier_semaphore()
    for d in range(1, 4):
        pl.semaphore_signal(
            barrier, inc=1, device_id=(i, (j + d) % 4), device_id_type=pl.DeviceIdType.MESH
        )
    for d in range(1, 8):
        pl.semaphore_signal(
            barrier, inc=1, device_id=((i + d) % 8, j), device_id_type=pl.DeviceIdType.MESH
        )
    pl.semaphore_wait(barrier, 10)

    sent = []
    diag_copies = []
    part_copies = []
    right_copies = []
    for d in range(1, 4):
        there = (j + d) % 4
        diag_copies.append(to(diag_ref.at[there], diag_in.at[d - 1], diag_sem.at[d - 1], i, there))
        diag_copies[-1].start()
    for d in range(1, 4):
        there = (j + d) % 4
        part_copies.append(to(parts_ref.at[there], parts_in.at[d - 1], part_sem.at[d - 1], i, there))
        part_copies[-1].start()
    right_all[i] = right_ref[...]
    for d in range(1, 8):
        right_copies.append(
            to(right_all.at[i], right_all.at[i], right_sem.at[d - 1], (i + d) % 8, j)
        )
        right_copies[-1].start()

    total = diag_ref[j]
    for d in range(3):
        diag_copies[d].wait()
        total = total + diag_in[d]
    diag_all[i] = total
    row_copies = []
    for d in range(1, 8):
        row_copies.append(to(diag_all.at[i], diag_all.at[i], row_sem.at[d - 1], (i + d) % 8, j))
        row_copies[-1].start()

    for d in range(3):
        part_copies[d].wait()
    piece = parts_ref[j] + parts_in[0] + parts_in[1] + parts_in[2]
    columns_ref[i] = piece
    own_ref[j] = piece

    def ring_copy(step, way):
        origin = ring_index((place + (8 - step if way == 0 else step)) % 8)
        target = after if way == 0 else before
        spot = columns_ref.at[origin, pl.ds(way * half, half)]
        return to(spot, spot, ring_sem.at[way, step], target, j)

    def ring_arrival(step, way):
        origin = ring_index((place + (7 - step if way == 0 else step + 1)) % 8)
        spot = columns_ref.at[origin, pl.ds(way * half, half)]
        return to(spot, spot, ring_sem.at[way, step], after if way == 0 else before, j)

    def ring_step(step):
        for way in range(2):
            ring_arrival(step - 1, way).wait_recv()
            ring_copy(step, way).start()

    for way in range(2):
        ring_copy(0, way).start()
    own_copies = []
    for d in range(1, 4):
        own_copies.append(to(own_ref.at[j], own_ref.at[j], own_sem.at[d - 1], i, (j + d) % 4))
        own_copies[-1].start()

    def arrival(buffer, sems, d):
        here = (i + 8 - d) % 8
        return to(buffer.at[here], buffer.at[here], sems.at[d - 1], here, j)

    for d in range(1, 8):
        arrival(diag_all, row_sem, d).wait_recv()
    for q in range(4):
        both = diag_all[q] + diag_all[q + 4]
        for panel in range(PANELS):
            slabs[j, panel * PW + q * block_rows : panel * PW + (q + 1) * block_rows, :] = both[
                panel * block_rows : (panel + 1) * block_rows, :
            ]
    slab_copies = []
    for d in range(1, 4):
        slab_copies.append(to(slabs.at[j], slabs.at[j], slab_sem.at[d - 1], i, (j + d) % 4))
        slab_copies[-1].start()
    ring_step(1)
    for d in range(1, 8):
        arrival(right_all, right_sem, d).wait_recv()
    for q in range(4):
        both = right_all[q] + right_all[q + 4]
        for panel in range(PANELS):
            wanted_ref[panel * PW + q * block_rows : panel * PW + (q + 1) * block_rows, :] = both[
                panel * block_rows : (panel + 1) * block_rows, :
            ]
    for d in range(1, 4):
        here = (j + 4 - d) % 4
        to(slabs.at[here], slabs.at[here], slab_sem.at[d - 1], i, here).wait_recv()
    for q in range(4):
        work[:, q * SUB : (q + 1) * SUB] = slabs[q]
    ring_step(2)

    def between(k, turn):
        @pl.when(k < 2)
        def _():
            ring_step(3 + 2 * k + turn)

    invert_steps(work, between)
    out_ref[...] = work[:, WIDE:]

    for way in range(2):
        ring_arrival(6, way).wait_recv()
        for step in range(7):
            ring_copy(step, way).wait_send()
    for d in range(1, 4):
        here = (j + 4 - d) % 4
        to(own_ref.at[here], own_ref.at[here], own_sem.at[d - 1], i, here).wait_recv()
    for copy in own_copies + slab_copies + row_copies + right_copies:
        copy.wait_send()


def exchange(parts, diag, right):
    share = parts.shape[1]
    rights = right.shape[1]
    whole = pl.BlockSpec(memory_space=pltpu.VMEM)
    sems = pltpu.SemaphoreType.DMA
    return pl.pallas_call(
        exchange_kernel,
        in_specs=[whole] * 3,
        out_specs=[whole] * 4,
        out_shape=[
            jax.ShapeDtypeStruct(parts.shape, jnp.float32),
            jax.ShapeDtypeStruct((8, share, WIDE), jnp.float32),
            jax.ShapeDtypeStruct((WIDE, rights), jnp.float32),
            jax.ShapeDtypeStruct((WIDE, WIDE), jnp.float32),
        ],
        scratch_shapes=[
            pltpu.VMEM((3, share, WIDE), jnp.float32),
            pltpu.VMEM((3, SUB, SUB), jnp.float32),
            pltpu.VMEM((8, SUB, SUB), jnp.float32),
            pltpu.VMEM((8, SUB, rights), jnp.float32),
            pltpu.VMEM((4, WIDE, SUB), jnp.float32),
            pltpu.VMEM((WIDE, 2 * WIDE), jnp.float32),
            sems((3, 2)), sems((3, 2)), sems((7, 2)), sems((7, 2)), sems((3, 2)), sems((3, 2)),
            sems((2, 7, 2)),
        ],
        compiler_params=pltpu.CompilerParams(
            collective_id=0, has_side_effects=True, vmem_limit_bytes=48 * 1024 * 1024
        ),
        name="exchange",
    )(parts, diag, right)


def halves(value):
    high = value.astype(jnp.bfloat16)
    low = (value - high.astype(jnp.float32)).astype(jnp.bfloat16)
    return high, low


def times_transposed(left, right):
    return lax.dot_general(
        left,
        right,
        (((1,), (1,)), ((), ())),
        precision=EXACT,
        preferred_element_type=jnp.float32,
    )


def split_product(left, right):
    def one(a, b):
        return lax.dot_general(
            a, b, (((1,), (1,)), ((), ())), preferred_element_type=jnp.float32
        )

    return one(left[0], right[0]) + (one(left[0], right[1]) + one(left[1], right[0]))


def update_kernel(
    inverse_ref, wanted_ref, cols_ref, own_ref, kernel_ref, samples_ref,
    trailing_ref, factor_ref, solved_ref, reduced_ref,
    own_high, own_low, cols_high, cols_low,
):
    j = pl.program_id(0)
    i = pl.program_id(1)
    tile = kernel_ref.shape[0]
    at = pl.ds(pl.multiple_of(i * tile, tile), tile)

    @pl.when((i == 0) & (j == 0))
    def _():
        solved_ref[...] = jnp.dot(
            inverse_ref[...], wanted_ref[...], precision=EXACT, preferred_element_type=jnp.float32
        )

    @pl.when(i == 0)
    def _():
        columns = cols_ref[...].swapaxes(0, 1).reshape(cols_high.shape)
        high, low = halves(times_transposed(columns, inverse_ref[...]))
        cols_high[...] = high
        cols_low[...] = low

    @pl.when(j == 0)
    def _():
        factor = times_transposed(own_ref[...], inverse_ref[...])
        factor_ref[...] = factor
        high, low = halves(factor)
        own_high[at, :] = high
        own_low[at, :] = low
        reduced_ref[...] = samples_ref[...] - jnp.dot(
            factor, solved_ref[...], precision=EXACT, preferred_element_type=jnp.float32
        )

    trailing_ref[...] = kernel_ref[...] - split_product(
        (own_high[at, :], own_low[at, :]), (cols_high[...], cols_low[...])
    )


def update(inverse, wanted, columns, own, kernel, samples):
    rows, width = kernel.shape
    right = samples.shape[1]
    tile = min(512, rows)
    span = min(1024, width)
    steps = rows // tile
    groups, _, block_rows, _ = columns.shape
    runs = span // (groups * block_rows)

    def first(j, i):
        return (jnp.where(j == 0, i, steps - 1), 0)

    return pl.pallas_call(
        update_kernel,
        grid=(width // span, steps),
        in_specs=[
            pl.BlockSpec((WIDE, WIDE), lambda j, i: (0, 0)),
            pl.BlockSpec((WIDE, right), lambda j, i: (0, 0)),
            pl.BlockSpec((groups, runs, block_rows, WIDE), lambda j, i: (0, j, 0, 0)),
            pl.BlockSpec((tile, WIDE), first),
            pl.BlockSpec((tile, span), lambda j, i: (i, j)),
            pl.BlockSpec((tile, right), first),
        ],
        out_specs=[
            pl.BlockSpec((tile, span), lambda j, i: (i, j)),
            pl.BlockSpec((tile, WIDE), first),
            pl.BlockSpec((WIDE, right), lambda j, i: (0, 0)),
            pl.BlockSpec((tile, right), first),
        ],
        out_shape=[
            jax.ShapeDtypeStruct((rows, width), jnp.float32),
            jax.ShapeDtypeStruct((rows, WIDE), jnp.float32),
            jax.ShapeDtypeStruct((WIDE, right), jnp.float32),
            jax.ShapeDtypeStruct((rows, right), jnp.float32),
        ],
        scratch_shapes=[
            pltpu.VMEM((rows, WIDE), jnp.bfloat16),
            pltpu.VMEM((rows, WIDE), jnp.bfloat16),
            pltpu.VMEM((span, WIDE), jnp.bfloat16),
            pltpu.VMEM((span, WIDE), jnp.bfloat16),
        ],
        compiler_params=pltpu.CompilerParams(vmem_limit_bytes=56 * 1024 * 1024),
        name="update",
    )(inverse, wanted, columns, own, kernel, samples)


def on_device(kernel, row_block, panel_order, samples):
    rows_count = lax.axis_size("rows")
    cols_count = lax.axis_size("cols")
    cols_place = lax.axis_index("cols")
    blocks_here = row_block.shape[0]
    local_rows, local_cols = kernel.shape
    block_rows = local_rows // blocks_here
    per_panel = PW // block_rows
    share = blocks_here // cols_count
    right_cols = samples.shape[1]
    ranking = jnp.argsort(row_block)

    picked = []
    wanted = []
    for step in range(PANELS):
        start = panel_order[step] * PW
        owner = start // local_cols
        part = lax.dynamic_slice_in_dim(kernel, start - owner * local_cols, PW, 1)
        picked.append(jnp.where(cols_place == owner, part, jnp.zeros_like(part)))
        wanted.append(panel_order[step] * per_panel + jnp.arange(per_panel, dtype=jnp.int32))
    picked = jnp.concatenate(picked, 1).reshape(blocks_here, block_rows, WIDE)
    sample_blocks = samples.reshape(blocks_here, block_rows, right_cols)

    def held_rows(blocks, names):
        matches = names[:, None] == row_block[None, :]
        held = jnp.any(matches, 1)[:, None, None]
        found = jnp.where(held, jnp.take(blocks, jnp.argmax(matches, 1), axis=0), 0.0)
        return found.reshape(-1, blocks.shape[2])

    if (rows_count, cols_count) == (8, 4) and per_panel == 4:
        place = lax.axis_index("rows") % per_panel
        names = jnp.stack([panel_order[step] * per_panel + place for step in range(PANELS)])
        parts = jnp.take(picked, ranking, axis=0).reshape(cols_count, share * block_rows, WIDE)
        diag = held_rows(picked, names).reshape(-1, cols_count, SUB).transpose(1, 0, 2)
        right = held_rows(sample_blocks, names)
        own, columns, panel_right, inverse = exchange(parts, diag, right)
        own = jnp.take(
            own.reshape(blocks_here, block_rows, WIDE), row_block // rows_count, axis=0
        ).reshape(local_rows, WIDE)
        columns = columns.reshape(rows_count, share, block_rows, WIDE)
    else:
        names = jnp.concatenate(wanted, 0)
        own_blocks = lax.psum(picked, "cols")
        own = own_blocks.reshape(local_rows, WIDE)
        diagonal, panel_right = lax.psum(
            (held_rows(own_blocks, names), held_rows(sample_blocks, names)), "rows"
        )
        mine = lax.dynamic_slice_in_dim(ranking, cols_place * share, share, 0)
        columns = lax.all_gather(jnp.take(own_blocks, mine, axis=0), "rows", axis=0)
        columns = columns.transpose(1, 0, 2, 3).reshape(1, -1, block_rows, WIDE)
        inverse = invert(diagonal)
    return tuple(update(inverse, panel_right, columns, own, kernel, samples))


def solution(mesh):
    in_specs = (P("rows", "cols"), P("rows"), P(), P("rows", "cols"))
    out_specs = (P("rows", "cols"), P("rows", None), P(None, "cols"), P("rows", "cols"))
    return jax.shard_map(
        on_device, mesh=mesh, in_specs=in_specs, out_specs=out_specs, check_vma=False
    )
```

```python
import functools

import jax
import jax.numpy as jnp
from jax import lax
from jax.experimental import pallas as pl
from jax.experimental.pallas import tpu as pltpu
from jax.sharding import PartitionSpec as P

PW = 256
PANELS = 2
WIDE = PW * PANELS
SUB = 128
STRIP = 16

EXACT = lax.Precision.HIGHEST


def eliminate(block):
    strips = [block[s * STRIP : (s + 1) * STRIP, :] for s in range(SUB // STRIP)]
    place = lax.broadcasted_iota(jnp.int32, (STRIP, 1), 0)
    lane = lax.broadcasted_iota(jnp.int32, (1, SUB), 1)
    for col in range(SUB):
        home, spot = divmod(col, STRIP)
        row = strips[home][spot : spot + 1, :]
        scale = 1.0 / row[:, col : col + 1]
        scaled = jnp.where(lane == col, 1.0 + scale, row * scale)
        for s in range(home, SUB // STRIP):
            ratio = strips[s][:, col : col + 1]
            if s == home:
                ratio = jnp.where(place > spot, ratio, 0.0)
            strips[s] = strips[s] - ratio * scaled
    merged = jnp.concatenate(strips, axis=0)
    rows = lax.broadcasted_iota(jnp.int32, (SUB, SUB), 0)
    lanes = lax.broadcasted_iota(jnp.int32, (SUB, SUB), 1)
    pivots = jnp.sum(jnp.where(rows == lanes, merged, 0.0), axis=1, keepdims=True)
    lower = jnp.where(rows > lanes, merged, jnp.where(rows == lanes, 1.0, 0.0))
    return lower * lax.rsqrt(pivots)


def invert_steps(work, between):
    count = WIDE // SUB
    rows = lax.broadcasted_iota(jnp.int32, (WIDE, WIDE), 0)
    lanes = lax.broadcasted_iota(jnp.int32, (WIDE, WIDE), 1)
    work[:, WIDE:] = jnp.where(rows == lanes, 1.0, 0.0).astype(jnp.float32)

    def step(k, carry):
        here = pl.ds(pl.multiple_of(k * SUB, SUB), SUB)
        inverse = eliminate(work[here, here])
        between(k)
        work[here, :] = jnp.dot(
            inverse, work[here, :], precision=EXACT, preferred_element_type=jnp.float32
        )
        for i in range(1, count):

            @pl.when(i > k)
            def _():
                work[i * SUB : (i + 1) * SUB, :] -= lax.dot_general(
                    work[here, i * SUB : (i + 1) * SUB],
                    work[here, :],
                    (((0,), (0,)), ((), ())),
                    precision=EXACT,
                    preferred_element_type=jnp.float32,
                )

        return carry

    lax.fori_loop(0, count, step, 0)


def invert_kernel(diag_ref, out_ref, work):
    work[:, :WIDE] = diag_ref[...]
    invert_steps(work, lambda k: None)
    out_ref[...] = work[:, WIDE:]


def invert(diagonal):
    return pl.pallas_call(
        invert_kernel,
        out_shape=jax.ShapeDtypeStruct((WIDE, WIDE), jnp.float32),
        in_specs=[pl.BlockSpec(memory_space=pltpu.VMEM)],
        out_specs=pl.BlockSpec(memory_space=pltpu.VMEM),
        scratch_shapes=[pltpu.VMEM((WIDE, 2 * WIDE), jnp.float32)],
        compiler_params=pltpu.CompilerParams(vmem_limit_bytes=32 * 1024 * 1024),
        name="invert",
    )(diagonal)


def ring_index(position):
    turn = position // 4
    return 2 * (position + turn * (7 - 2 * position)) + turn


def exchange_kernel(
    parts_ref, diag_ref, right_ref,
    own_ref, columns_ref, wanted_ref, out_ref,
    parts_in, diag_in, diag_all, right_all, slabs, work,
    part_sem, diag_sem, row_sem, right_sem, slab_sem, own_sem, ring_sem,
):
    i = lax.axis_index("rows")
    j = lax.axis_index("cols")
    place = (i // 2) + (i % 2) * (7 - 2 * (i // 2))
    after = ring_index((place + 1) % 8)
    before = ring_index((place + 7) % 8)
    half = columns_ref.shape[1] // 2
    rights = right_ref.shape[1]
    block_rows = SUB // PANELS

    def to(src, dst, sems, row, col):
        return pltpu.make_async_remote_copy(
            src_ref=src, dst_ref=dst, send_sem=sems.at[0], recv_sem=sems.at[1],
            device_id=(row, col), device_id_type=pl.DeviceIdType.MESH,
        )

    barrier = pltpu.get_barrier_semaphore()
    for d in range(1, 4):
        pl.semaphore_signal(
            barrier, inc=1, device_id=(i, (j + d) % 4), device_id_type=pl.DeviceIdType.MESH
        )
    for d in range(1, 8):
        pl.semaphore_signal(
            barrier, inc=1, device_id=((i + d) % 8, j), device_id_type=pl.DeviceIdType.MESH
        )
    pl.semaphore_wait(barrier, 10)

    sent = []
    diag_copies = []
    part_copies = []
    right_copies = []
    for d in range(1, 4):
        there = (j + d) % 4
        diag_copies.append(to(diag_ref.at[there], diag_in.at[d - 1], diag_sem.at[d - 1], i, there))
        diag_copies[-1].start()
    for d in range(1, 4):
        there = (j + d) % 4
        part_copies.append(to(parts_ref.at[there], parts_in.at[d - 1], part_sem.at[d - 1], i, there))
        part_copies[-1].start()
    right_all[i] = right_ref[...]
    for d in range(1, 8):
        right_copies.append(
            to(right_all.at[i], right_all.at[i], right_sem.at[d - 1], (i + d) % 8, j)
        )
        right_copies[-1].start()

    total = diag_ref[j]
    for d in range(3):
        diag_copies[d].wait()
        total = total + diag_in[d]
    diag_all[i] = total
    row_copies = []
    for d in range(1, 8):
        row_copies.append(to(diag_all.at[i], diag_all.at[i], row_sem.at[d - 1], (i + d) % 8, j))
        row_copies[-1].start()

    for d in range(3):
        part_copies[d].wait()
    piece = parts_ref[j] + parts_in[0] + parts_in[1] + parts_in[2]
    columns_ref[i] = piece
    own_ref[j] = piece

    def ring_copy(step, way):
        origin = ring_index((place + (8 - step if way == 0 else step)) % 8)
        target = after if way == 0 else before
        spot = columns_ref.at[origin, pl.ds(way * half, half)]
        return to(spot, spot, ring_sem.at[way, step], target, j)

    def ring_arrival(step, way):
        origin = ring_index((place + (7 - step if way == 0 else step + 1)) % 8)
        spot = columns_ref.at[origin, pl.ds(way * half, half)]
        return to(spot, spot, ring_sem.at[way, step], after if way == 0 else before, j)

    def ring_step(step):
        for way in range(2):
            ring_arrival(step - 1, way).wait_recv()
            ring_copy(step, way).start()

    for way in range(2):
        ring_copy(0, way).start()
    own_copies = []
    for d in range(1, 4):
        own_copies.append(to(own_ref.at[j], own_ref.at[j], own_sem.at[d - 1], i, (j + d) % 4))
        own_copies[-1].start()

    def arrival(buffer, sems, d):
        here = (i + 8 - d) % 8
        return to(buffer.at[here], buffer.at[here], sems.at[d - 1], here, j)

    for d in range(1, 8):
        arrival(diag_all, row_sem, d).wait_recv()
    for q in range(4):
        both = diag_all[q] + diag_all[q + 4]
        for panel in range(PANELS):
            slabs[j, panel * PW + q * block_rows : panel * PW + (q + 1) * block_rows, :] = both[
                panel * block_rows : (panel + 1) * block_rows, :
            ]
    slab_copies = []
    for d in range(1, 4):
        slab_copies.append(to(slabs.at[j], slabs.at[j], slab_sem.at[d - 1], i, (j + d) % 4))
        slab_copies[-1].start()
    ring_step(1)
    for d in range(1, 8):
        arrival(right_all, right_sem, d).wait_recv()
    for q in range(4):
        both = right_all[q] + right_all[q + 4]
        for panel in range(PANELS):
            wanted_ref[panel * PW + q * block_rows : panel * PW + (q + 1) * block_rows, :] = both[
                panel * block_rows : (panel + 1) * block_rows, :
            ]
    for d in range(1, 4):
        here = (j + 4 - d) % 4
        to(slabs.at[here], slabs.at[here], slab_sem.at[d - 1], i, here).wait_recv()
    for q in range(4):
        work[:, q * SUB : (q + 1) * SUB] = slabs[q]
    ring_step(2)

    invert_steps(work, lambda k: ring_step(3 + k))
    out_ref[...] = work[:, WIDE:]

    for way in range(2):
        ring_arrival(6, way).wait_recv()
        for step in range(7):
            ring_copy(step, way).wait_send()
    for d in range(1, 4):
        here = (j + 4 - d) % 4
        to(own_ref.at[here], own_ref.at[here], own_sem.at[d - 1], i, here).wait_recv()
    for copy in own_copies + slab_copies + row_copies + right_copies:
        copy.wait_send()


def exchange(parts, diag, right):
    share = parts.shape[1]
    rights = right.shape[1]
    whole = pl.BlockSpec(memory_space=pltpu.VMEM)
    sems = pltpu.SemaphoreType.DMA
    return pl.pallas_call(
        exchange_kernel,
        in_specs=[whole] * 3,
        out_specs=[whole] * 4,
        out_shape=[
            jax.ShapeDtypeStruct(parts.shape, jnp.float32),
            jax.ShapeDtypeStruct((8, share, WIDE), jnp.float32),
            jax.ShapeDtypeStruct((WIDE, rights), jnp.float32),
            jax.ShapeDtypeStruct((WIDE, WIDE), jnp.float32),
        ],
        scratch_shapes=[
            pltpu.VMEM((3, share, WIDE), jnp.float32),
            pltpu.VMEM((3, SUB, SUB), jnp.float32),
            pltpu.VMEM((8, SUB, SUB), jnp.float32),
            pltpu.VMEM((8, SUB, rights), jnp.float32),
            pltpu.VMEM((4, WIDE, SUB), jnp.float32),
            pltpu.VMEM((WIDE, 2 * WIDE), jnp.float32),
            sems((3, 2)), sems((3, 2)), sems((7, 2)), sems((7, 2)), sems((3, 2)), sems((3, 2)),
            sems((2, 7, 2)),
        ],
        compiler_params=pltpu.CompilerParams(
            collective_id=0, has_side_effects=True, vmem_limit_bytes=48 * 1024 * 1024
        ),
        name="exchange",
    )(parts, diag, right)


def halves(value):
    high = value.astype(jnp.bfloat16)
    low = (value - high.astype(jnp.float32)).astype(jnp.bfloat16)
    return high, low


def times_transposed(left, right):
    return lax.dot_general(
        left,
        right,
        (((1,), (1,)), ((), ())),
        precision=EXACT,
        preferred_element_type=jnp.float32,
    )


def update_kernel(
    inverse_ref, wanted_ref, cols_ref, own_ref, kernel_ref, samples_ref,
    trailing_ref, factor_ref, solved_ref, reduced_ref,
    own_halves, cols_halves,
):
    j = pl.program_id(0)
    i = pl.program_id(1)
    tile = kernel_ref.shape[0]
    at = pl.ds(pl.multiple_of(i * tile, tile), tile)

    @pl.when((i == 0) & (j == 0))
    def _():
        solved_ref[...] = jnp.dot(
            inverse_ref[...], wanted_ref[...], precision=EXACT, preferred_element_type=jnp.float32
        )

    @pl.when(i == 0)
    def _():
        columns = cols_ref[...].swapaxes(0, 1).reshape(-1, WIDE)
        high, low = halves(times_transposed(inverse_ref[...], columns))
        cols_halves[:WIDE, :] = high
        cols_halves[WIDE : 2 * WIDE, :] = low
        cols_halves[2 * WIDE :, :] = high

    @pl.when(j == 0)
    def _():
        factor = times_transposed(own_ref[...], inverse_ref[...])
        factor_ref[...] = factor
        high, low = halves(factor)
        own_halves[at, :WIDE] = high
        own_halves[at, WIDE : 2 * WIDE] = high
        own_halves[at, 2 * WIDE :] = low
        reduced_ref[...] = samples_ref[...] - jnp.dot(
            factor, solved_ref[...], precision=EXACT, preferred_element_type=jnp.float32
        )

    trailing_ref[...] = kernel_ref[...] - jnp.dot(
        own_halves[at, :], cols_halves[...], preferred_element_type=jnp.float32
    )


def update(inverse, wanted, columns, own, kernel, samples):
    rows, width = kernel.shape
    right = samples.shape[1]
    tile = min(512, rows)
    span = min(1024, width)
    steps = rows // tile
    groups, _, block_rows, _ = columns.shape
    runs = span // (groups * block_rows)

    def first(j, i):
        return (jnp.where(j == 0, i, steps - 1), 0)

    return pl.pallas_call(
        update_kernel,
        grid=(width // span, steps),
        in_specs=[
            pl.BlockSpec((WIDE, WIDE), lambda j, i: (0, 0)),
            pl.BlockSpec((WIDE, right), lambda j, i: (0, 0)),
            pl.BlockSpec((groups, runs, block_rows, WIDE), lambda j, i: (0, j, 0, 0)),
            pl.BlockSpec((tile, WIDE), first),
            pl.BlockSpec((tile, span), lambda j, i: (i, j)),
            pl.BlockSpec((tile, right), first),
        ],
        out_specs=[
            pl.BlockSpec((tile, span), lambda j, i: (i, j)),
            pl.BlockSpec((tile, WIDE), first),
            pl.BlockSpec((WIDE, right), lambda j, i: (0, 0)),
            pl.BlockSpec((tile, right), first),
        ],
        out_shape=[
            jax.ShapeDtypeStruct((rows, width), jnp.float32),
            jax.ShapeDtypeStruct((rows, WIDE), jnp.float32),
            jax.ShapeDtypeStruct((WIDE, right), jnp.float32),
            jax.ShapeDtypeStruct((rows, right), jnp.float32),
        ],
        scratch_shapes=[
            pltpu.VMEM((rows, 3 * WIDE), jnp.bfloat16),
            pltpu.VMEM((3 * WIDE, span), jnp.bfloat16),
        ],
        compiler_params=pltpu.CompilerParams(vmem_limit_bytes=56 * 1024 * 1024),
        name="update",
    )(inverse, wanted, columns, own, kernel, samples)


def on_device(kernel, row_block, panel_order, samples):
    rows_count = lax.axis_size("rows")
    cols_count = lax.axis_size("cols")
    cols_place = lax.axis_index("cols")
    blocks_here = row_block.shape[0]
    local_rows, local_cols = kernel.shape
    block_rows = local_rows // blocks_here
    per_panel = PW // block_rows
    share = blocks_here // cols_count
    right_cols = samples.shape[1]
    ranking = jnp.argmax(
        (row_block // rows_count)[None, :] == jnp.arange(blocks_here, dtype=jnp.int32)[:, None], 1
    )

    picked = []
    wanted = []
    for step in range(PANELS):
        start = panel_order[step] * PW
        owner = start // local_cols
        part = lax.dynamic_slice_in_dim(kernel, start - owner * local_cols, PW, 1)
        picked.append(jnp.where(cols_place == owner, part, jnp.zeros_like(part)))
        wanted.append(panel_order[step] * per_panel + jnp.arange(per_panel, dtype=jnp.int32))
    picked = jnp.concatenate(picked, 1).reshape(blocks_here, block_rows, WIDE)
    sample_blocks = samples.reshape(blocks_here, block_rows, right_cols)

    def held_rows(blocks, names):
        matches = names[:, None] == row_block[None, :]
        held = jnp.any(matches, 1)[:, None, None]
        found = jnp.where(held, jnp.take(blocks, jnp.argmax(matches, 1), axis=0, mode="clip"), 0.0)
        return found.reshape(-1, blocks.shape[2])

    if (rows_count, cols_count) == (8, 4) and per_panel == 4:
        place = lax.axis_index("rows") % per_panel
        names = jnp.stack([panel_order[step] * per_panel + place for step in range(PANELS)])
        parts = jnp.take(picked, ranking, axis=0, mode="clip").reshape(cols_count, share * block_rows, WIDE)
        diag = held_rows(picked, names).reshape(-1, cols_count, SUB).transpose(1, 0, 2)
        right = held_rows(sample_blocks, names)
        own, columns, panel_right, inverse = exchange(parts, diag, right)
        own = jnp.take(
            own.reshape(blocks_here, block_rows, WIDE), row_block // rows_count, axis=0, mode="clip"
        ).reshape(local_rows, WIDE)
        columns = columns.reshape(rows_count, share, block_rows, WIDE)
    else:
        names = jnp.concatenate(wanted, 0)
        own_blocks = lax.psum(picked, "cols")
        own = own_blocks.reshape(local_rows, WIDE)
        diagonal, panel_right = lax.psum(
            (held_rows(own_blocks, names), held_rows(sample_blocks, names)), "rows"
        )
        mine = lax.dynamic_slice_in_dim(ranking, cols_place * share, share, 0)
        columns = lax.all_gather(jnp.take(own_blocks, mine, axis=0, mode="clip"), "rows", axis=0)
        columns = columns.transpose(1, 0, 2, 3).reshape(1, -1, block_rows, WIDE)
        inverse = invert(diagonal)
    return tuple(update(inverse, panel_right, columns, own, kernel, samples))


def solution(mesh):
    in_specs = (P("rows", "cols"), P("rows"), P(), P("rows", "cols"))
    out_specs = (P("rows", "cols"), P("rows", None), P(None, "cols"), P("rows", "cols"))
    return jax.shard_map(
        on_device, mesh=mesh, in_specs=in_specs, out_specs=out_specs, check_vma=False
    )
```
